256 devices in a mesh: rep: 8 (over z_lo, core), fsdp: 32 (over z_hi, y, x).
Axes of the slice: x: 4, y: 4, z: 8 (z_hi: 2, z_lo: 4; z = z_hi * 4 + z_lo), core: 2. Of those that a mesh axis runs over, the one named last changes fastest.
Arguments:
- activations: bfloat16 [8, 24576, 6144], P('rep', 'fsdp'), may hold values from -6 to 6
- out_grads: bfloat16 [8, 24576, 512], P('rep', 'fsdp'), may hold values from -0.0390625 to 0.0390625
- momentum: float32 [8, 6144, 512], P('rep', 'fsdp'), may hold values from -6 to 6
- band: int32 [512], replicated, may hold values from 0 to 4095, as said below
Outputs:
- update: float32 [6144, 512], P('fsdp')
- new_momentum: float32 [8, 6144, 512], P('rep', 'fsdp')
The draws below stay inside these ranges and needn't reach their ends.
Inputs may be any that keep to these rules, and one draw needn't show every extreme that they name: `band`: distinct positions in a group's flattened coefficients; 0 and 4095 are always among them.
All inputs are finite; a program needn't handle non-finite values.
Results may differ from the reference program's by a relative error of at most 0.0003.
Values may be sent and summed in bfloat16 or wider, within the bound.
No kernel may reach another device: no remote copies, remote signals or barrier semaphores. Data moves between devices by JAX's collectives and lax.ppermute only.
A program may use at most 128 MiB of HBM per device.

```python
import jax
import jax.numpy as jnp
from jax import lax

D = 6144
KV = 512
GROUP = 64
BAND = 512
TOKENS = 24576
REPS = 8


def draw_band(key, part):
    key = jax.random.fold_in(key, 11)
    first_key, second_key = jax.random.split(key)
    inner = jax.random.permutation(first_key, GROUP * GROUP - 2)[:BAND - 2] + 1
    ends = jnp.array([0, GROUP * GROUP - 1], jnp.int32)
    joined = jnp.concatenate([inner.astype(jnp.int32), ends])
    return jax.random.permutation(second_key, joined).astype(jnp.int32)


def levels(stream_key, dims, shards, low, largest):
    gain, own = 1.0, jax.random.fold_in(stream_key, 6)
    for position, shards_of in shards:
        heights = jnp.exp(jax.random.uniform(jax.random.fold_in(own, position), (shards_of,), jnp.float32, low / len(shards), largest / len(shards)))
        gain = gain * jnp.repeat(heights, dims[position] // shards_of).reshape([-1 if axis == position else 1 for axis in range(len(dims))])
    return gain


def scatter_about(rng, shape, width, most, cuts=(), held_as=jnp.bfloat16):
    gain = levels(rng, shape, cuts, -0.22, 0.18) if cuts else 1.0
    values = jax.random.normal(rng, shape, jnp.float32) * width * gain
    return jnp.minimum(jnp.maximum(values, -most), most).astype(held_as)


def setup_inputs(seed: int = 0) -> dict:
    key_list = jax.random.split(jax.random.key(seed), 5)
    return {
        "activations": scatter_about(key_list[0], (REPS, TOKENS, D), 1.0, 6.0, ((0, 8), (1, 32))),
        "out_grads": scatter_about(key_list[1], (REPS, TOKENS, KV), TOKENS ** -0.5, 0.0390625, ((0, 8), (1, 32))),
        "momentum": scatter_about(key_list[2], (REPS, D, KV), 1.0, 6.0, ((0, 8), (1, 32)), jnp.float32),
        "band": draw_band(jax.random.fold_in(key_list[4], 71), 0),
    }


decay_rate = 0.999

def dct_table(order):
    steps = jnp.arange(order, dtype=jnp.float32)
    waves = jnp.cos(jnp.pi * (2.0 * steps[None, :] + 1.0) * steps[:, None] / (2.0 * order))
    waves = waves * jnp.sqrt(jnp.float32(2.0 / order))
    first = jnp.where(steps == 0, jnp.float32(0.5) ** 0.5, jnp.float32(1.0))
    return waves * first[:, None]

def to_groups(matrix):
    return matrix.reshape(D // GROUP, GROUP, KV // GROUP, GROUP).transpose(0, 2, 1, 3)

def from_groups(blocks):
    return blocks.transpose(0, 2, 1, 3).reshape(D, KV)

def to_coeffs(matrix, table):
    blocks = jnp.einsum('ai,rcij,bj->rcab', table, to_groups(matrix), table, precision=lax.Precision.HIGHEST)
    return blocks.reshape(D // GROUP, KV // GROUP, GROUP * GROUP)

def from_band(values, band, table):
    full = jnp.zeros((D // GROUP, KV // GROUP, GROUP * GROUP), jnp.float32).at[:, :, band].set(values)
    blocks = full.reshape(D // GROUP, KV // GROUP, GROUP, GROUP)
    back = jnp.einsum('ia,rcij,jb->rcab', table, blocks, table, precision=lax.Precision.HIGHEST)
    return from_groups(back)

def reference(activations, out_grads, momentum, band):
    table = dct_table(GROUP)

    def one_replica(replica):
        acts = activations[replica].astype(jnp.float32)
        grad_out = out_grads[replica].astype(jnp.float32)
        grad = jnp.dot(acts.T, grad_out, precision=lax.Precision.HIGHEST)
        mom_now = decay_rate * momentum[replica] + grad
        kept = to_coeffs(mom_now, table)[:, :, band]
        return (mom_now, kept)
    moms, kepts = lax.map(one_replica, jnp.arange(REPS, dtype=jnp.int32))
    shared = lax.optimization_barrier(jnp.sum(kepts, axis=0)) / REPS
    update = from_band(shared, band, table)

    def remove_sent(replica):
        return moms[replica] - from_band(kepts[replica], band, table)
    new_momentum = lax.map(remove_sent, jnp.arange(REPS, dtype=jnp.int32))
    return (update, new_momentum)
```

```python
import functools

import jax
import jax.numpy as jnp
import numpy as np
from jax import lax
from jax.experimental import pallas as pl
from jax.experimental.pallas import tpu as pltpu
from jax.sharding import PartitionSpec as P

GROUP = 64
REPS = 8
DECAY = 0.999
HEAD = 16
STEPS = 256.0
TOP = 32766.0
LIMIT = 56 << 20
F32 = jnp.float32
I16 = jnp.int16
BF16 = jnp.bfloat16
CHAINS = ((1, 3), (3, 1))


def dct_table(order):
    n = np.arange(order)
    table = np.cos(np.pi * (2 * n[None, :] + 1) * n[:, None] / (2 * order)) * np.sqrt(2.0 / order)
    table[0] *= np.sqrt(0.5)
    return table.astype(np.float32)


def scale_code(biggest):
    top = jnp.max(biggest, axis=0, keepdims=True)
    return jnp.ceil(jnp.log2(jnp.maximum(top, 2.0**-110)) * STEPS)


def column_peak(x):
    return jnp.max(jnp.abs(x).reshape(x.shape[0] // 8, 8, x.shape[1]), axis=0)


def put_head(out, code):
    rows = jnp.broadcast_to(code, (HEAD, code.shape[1]))
    out[:HEAD, :] = rows.astype(jnp.int32).astype(I16)


def quantise(x, code):
    return jnp.round(x * (TOP * jnp.exp2(code * (-1.0 / STEPS)))).astype(jnp.int32).astype(I16)


def scale_of(msg):
    code = msg[:HEAD, :].astype(jnp.int32).astype(F32)[:1]
    return jnp.exp2(code * (1.0 / STEPS)) * (1.0 / TOP)


def dequantise(msg, block, rows, scale):
    return msg[HEAD + block * rows : HEAD + (block + 1) * rows, :].astype(jnp.int32).astype(F32) * scale


def partial_kernel(outs, late, passed, tabs, acts, og, *rest):
    n = len(outs)
    tab = tabs.at[late]
    rest = rest[passed:]
    out_refs = rest[:n]
    pieces, acc, peak, ready, in_sems, out_sems = rest[n + passed :]
    count, rows, half = acc.shape[2:]

    def fetch(i):
        first = pl.multiple_of(tab[0, i] * 2 * rows, 128)
        return pltpu.make_async_copy(acts.at[:, pl.ds(first, 2 * rows)], pieces.at[i], in_sems.at[i])

    for i in range(count):
        fetch(i).start()
    peak[...] = jnp.zeros_like(peak)

    @pl.loop(0, count)
    def _(i):
        fetch(i).wait()
        both = lax.dot_general(
            pieces[i], og[...], (((0,), (0,)), ((), ())), preferred_element_type=F32
        )
        for s in range(2):
            slot = tab[1 + s, i]
            part = both[s * rows : (s + 1) * rows]
            peak[slot] = jnp.maximum(peak[slot], column_peak(part))
            for c in range(2):
                place = tab[3 + 2 * c + s, i]
                acc[c, slot, place] = part[:, c * half : (c + 1) * half]
                for k, (k_slot, k_c, kind) in enumerate(outs):
                    if kind == "f" and k_c == c:

                        @pl.when(slot == k_slot)
                        def _():
                            pltpu.make_async_copy(
                                acc.at[c, k_slot, place], out_refs[k].at[place], out_sems.at[k]
                            ).start()

    copies = []
    for k, (slot, c, kind) in enumerate(outs):
        if kind == "f":
            copies.append(pltpu.make_async_copy(acc.at[c, slot], out_refs[k], out_sems.at[k]))
    q = 0
    for k, (slot, c, kind) in enumerate(outs):
        if kind == "q":
            out = ready.at[q]
            code = scale_code(peak[slot][:, c * half : (c + 1) * half])
            put_head(out, code)
            for b in range(count):
                out[HEAD + b * rows : HEAD + (b + 1) * rows, :] = quantise(acc[c, slot, b], code)
            copies.append(pltpu.make_async_copy(out, out_refs[k], out_sems.at[k]))
            copies[-1].start()
            q += 1
    for copy in copies:
        copy.wait()


def partials(outs, late, tab, acts, og, rows, through=()):
    tokens, _ = acts.shape
    width = og.shape[1]
    half = width // 2
    count = tab.shape[2]
    shapes = [
        jax.ShapeDtypeStruct((HEAD + count * rows, half), I16) if kind == "q" else f32(count, rows, half)
        for _, _, kind in outs
    ]
    messages = sum(kind == "q" for _, _, kind in outs)
    anywhere = pl.BlockSpec(memory_space=pl.ANY)
    return pl.pallas_call(
        functools.partial(partial_kernel, outs, late, len(through)),
        in_specs=[pl.BlockSpec(memory_space=pltpu.SMEM), anywhere, pl.BlockSpec(memory_space=pltpu.VMEM)]
        + [anywhere] * len(through),
        out_specs=[anywhere] * (len(outs) + len(through)),
        out_shape=shapes + [jax.ShapeDtypeStruct(t.shape, t.dtype) for t in through],
        input_output_aliases={3 + k: len(outs) + k for k in range(len(through))},
        scratch_shapes=[
            pltpu.VMEM((count, tokens, 2 * rows), BF16),
            pltpu.VMEM((2, 2, count, rows, half), F32),
            pltpu.VMEM((2, 8, width), F32),
            pltpu.VMEM((messages, HEAD + count * rows, half), I16),
            pltpu.SemaphoreType.DMA((count,)),
            pltpu.SemaphoreType.DMA((len(outs),)),
        ],
        compiler_params=pltpu.CompilerParams(vmem_limit_bytes=LIMIT),
        cost_estimate=pl.CostEstimate(
            flops=2 * tokens * count * 2 * rows * width, bytes_accessed=tokens * count * 2 * rows * 2, transcendentals=0
        ),
    )(tab, acts, og, *through)


def whole(shape, index=None):
    return pl.BlockSpec(shape, lambda i: index or (0,) * len(shape))


def call(kernel, ins, in_specs, outs, scratch=(), limit=16 << 20):
    total = sum(x.size * x.dtype.itemsize for x in ins) + sum(np.prod(o.shape) * o.dtype.itemsize for o in outs)
    return pl.pallas_call(
        kernel,
        grid=(1,),
        in_specs=in_specs,
        out_specs=[whole(o.shape) for o in outs],
        out_shape=outs,
        scratch_shapes=list(scratch),
        compiler_params=pltpu.CompilerParams(vmem_limit_bytes=limit),
        cost_estimate=pl.CostEstimate(flops=4 * int(total), bytes_accessed=int(total), transcendentals=0),
    )(*ins)


def i16(rows, width):
    return jax.ShapeDtypeStruct((HEAD + rows, width), I16)


def f32(*shape):
    return jax.ShapeDtypeStruct(shape, F32)


def second_kernel(own, first, out_a, out_b, held):
    rows = own.shape[1]
    quarter = own.shape[0] // 2
    scale = scale_of(first)
    for out, start in ((out_a, 0), (out_b, quarter)):
        peak = None
        for b in range(quarter):
            x = own[start + b] + dequantise(first, start + b, rows, scale)
            held[b] = x
            p = column_peak(x)
            peak = p if peak is None else jnp.maximum(peak, p)
        code = scale_code(peak)
        put_head(out, code)
        for b in range(quarter):
            out[HEAD + b * rows : HEAD + (b + 1) * rows, :] = quantise(held[b], code)


def third_kernel(own, near, far, out, held):
    rows = own.shape[1]
    n = own.shape[0]
    scale_n, scale_f = scale_of(near), scale_of(far)
    peak = None
    for b in range(n):
        x = own[b] + dequantise(near, b, rows, scale_n) + dequantise(far, b, rows, scale_f)
        held[b] = x
        p = column_peak(x)
        peak = p if peak is None else jnp.maximum(peak, p)
    code = scale_code(peak)
    put_head(out, code)
    for b in range(n):
        out[HEAD + b * rows : HEAD + (b + 1) * rows, :] = quantise(held[b], code)


def fourth_kernel(own, near, far, third, out, keep, held):
    rows = own.shape[1]
    n = own.shape[0]
    scale_n, scale_f, scale_t = scale_of(near), scale_of(far), scale_of(third)
    peak = None
    for b in range(n):
        x = own[b] + dequantise(near, n + b, rows, scale_n) + dequantise(far, b, rows, scale_f)
        x = x + dequantise(third, b, rows, scale_t)
        if b < n // 2:
            held[b] = x
            p = column_peak(x)
            peak = p if peak is None else jnp.maximum(peak, p)
        else:
            keep[b - n // 2] = x
    code = scale_code(peak)
    put_head(out, code)
    for b in range(n // 2):
        out[HEAD + b * rows : HEAD + (b + 1) * rows, :] = quantise(held[b], code)


def fifth_kernel(keep0, keep1, msg0, msg1, out, mine):
    rows = keep0.shape[1]
    half = keep0.shape[2]
    for c, (keep, msg) in enumerate(((keep0, msg0), (keep1, msg1))):
        cols = slice(c * half, (c + 1) * half)
        scale = scale_of(msg)
        mine[:, cols] = keep[0] + dequantise(msg, 0, rows, scale)
        x = keep[1] + dequantise(msg, 1, rows, scale)
        code = scale_code(column_peak(x))
        out[:HEAD, cols] = jnp.broadcast_to(code, (HEAD, half)).astype(jnp.int32).astype(I16)
        out[HEAD:, cols] = quantise(x, code)


def split(x):
    high = x.astype(BF16)
    return high, (x - high.astype(F32)).astype(BF16)


def mm(a, b):
    return jnp.dot(a, b, preferred_element_type=F32)


def waves_kernel(band, table, wa, wh, wl, th, tl):
    order = table.shape[0]
    n = band.shape[1]
    t = table[...]
    t0 = t.astype(BF16)
    r = t - t0.astype(F32)
    t1 = r.astype(BF16)
    t2 = (r - t1.astype(F32)).astype(BF16)
    ids = lax.broadcasted_iota(jnp.int32, (order, n), 0)
    pos = jnp.broadcast_to(band[...], (order, n))

    def pick(which):
        hot = jnp.where(ids == which, 1.0, 0.0).astype(BF16)
        return mm(t0, hot) + mm(t1, hot) + mm(t2, hot)

    left = pick(lax.shift_right_logical(pos, 6))
    right = pick(jnp.bitwise_and(pos, order - 1))
    for g in range(wa.shape[0] // order):
        wa[g * order : (g + 1) * order, :] = left
    high, low = split(right)
    for out, back, x in ((wh, th, high), (wl, tl, low)):
        x = x.astype(F32)
        zero = jnp.zeros_like(x)
        both = jnp.concatenate(
            [jnp.concatenate([x, zero], axis=1), jnp.concatenate([zero, x], axis=1)], axis=0
        )
        out[...] = both.astype(BF16)
        back[...] = both.T.astype(BF16)


def kept_kernel(mine, msg, momentum, wa, wh, wl, mom, kept):
    rows, width = mine.shape
    n = wa.shape[1]
    pairs = width // 128
    grad = mine[...] + msg[HEAD:, :].astype(jnp.int32).astype(F32) * scale_of(msg)
    now = DECAY * momentum[...] + grad
    mom[...] = now
    left = wa[...]
    for p in range(pairs):
        high, low = split(now[:, p * 128 : (p + 1) * 128])
        y = mm(high, wh[...]) + mm(low, wh[...]) + mm(high, wl[...])
        for h in range(2):
            z = left * y[:, h * n : (h + 1) * n]
            for g in range(rows // GROUP):
                row = g * 2 * pairs + 2 * p + h
                kept[row : row + 1, :] = jnp.sum(z[g * GROUP : (g + 1) * GROUP], axis=0, keepdims=True)


def back(values, wa, th, tl, store):
    n = wa.shape[1]
    groups = wa.shape[0] // GROUP
    pairs = values.shape[0] // groups // 2
    left = wa[:GROUP, :]
    for p in range(pairs):
        stacked = []
        for g in range(groups):
            row = g * 2 * pairs + 2 * p
            stacked.append(
                jnp.concatenate([left * values[row : row + 1], left * values[row + 1 : row + 2]], axis=1)
            )
        high, low = split(jnp.concatenate(stacked, axis=0))
        store(p, mm(high, th[...]) + mm(low, th[...]) + mm(high, tl[...]))


def momentum_kernel(mom, kept, wa, th, tl, out):
    def store(p, x):
        cols = slice(p * 128, (p + 1) * 128)
        out[:, cols] = mom[:, cols] - x

    back(kept[...], wa, th, tl, store)


def update_kernel(total, wa, th, tl, out):
    def store(p, x):
        out[:, p * 128 : (p + 1) * 128] = x

    back(total[...] * (1.0 / REPS), wa, th, tl, store)


def coords(f):
    return f // 16, (f // 4) % 4, f % 4


def partner_pairs(chain_step, late):
    pairs = []
    for rep in range(8):
        core = rep % 2
        for f in range(32):
            z, y, x = coords(f)
            if (core == 0) != late:
                x ^= chain_step
            else:
                y ^= chain_step
            pairs.append((rep * 32 + f, rep * 32 + z * 16 + y * 4 + x))
    return pairs


def far_pairs():
    return [(rep * 32 + f, rep * 32 + (f ^ 16)) for rep in range(8) for f in range(32)]


ORDERS = tuple((2, m1, m2, 0) for m1, m2 in CHAINS)


def tables():
    found = np.zeros((2, 32, 2, 7, 8), np.int32)
    for core in range(2):
        for f in range(32):
            z, y, x = coords(f)
            u, v = (x, y) if core == 0 else (y, x)
            for late in range(2):
                far_half = (u >> 1) ^ (1 - late)
                for i in range(8):
                    zr, a, b = i // 4, (i // 2) % 2, i % 2
                    yd, xh = (2 * a + b, far_half) if core == 0 else (2 * far_half + a, b)
                    column = [(z ^ zr) * 8 + yd * 2 + xh]
                    both = [((2 * xh + s, yd) if core == 0 else (yd, 2 * xh + s)) for s in range(2)]
                    column += [(ud ^ u) & 1 for ud, _ in both]
                    for order in ORDERS:
                        column += [order.index(vd ^ v) * 2 + zr for _, vd in both]
                    found[core, f, late, :, i] = column
    return found.reshape(64, 2, 7, 8)


def shards(activations, out_grads, momentum, band):
    acts, og, momentum = activations[0], out_grads[0], momentum[0]
    rows, width = momentum.shape
    half = width // 2
    axes = ("rep", "fsdp")
    core = lax.axis_index("rep") % 2
    place = core * 32 + lax.axis_index("fsdp")
    tab = lax.dynamic_index_in_dim(jnp.asarray(tables()), place, keepdims=False)

    table = jnp.asarray(dct_table(GROUP).T)
    n = band.shape[0]
    wa, wh, wl, th, tl = call(
        waves_kernel,
        (band.reshape(1, n), table),
        [whole((1, n)), whole((GROUP, GROUP))],
        [f32(rows, n)]
        + [jax.ShapeDtypeStruct((128, 2 * n), BF16)] * 2
        + [jax.ShapeDtypeStruct((2 * n, 128), BF16)] * 2,
    )

    def swap(x, step, late):
        return lax.ppermute(x, axes, partner_pairs(step, late))

    m1a0, m1a1, m1b1, own0 = partials(((0, 0, "q"), (0, 1, "q"), (1, 1, "q"), (1, 0, "f")), 0, tab, acts, og, rows)
    r1a = [swap(m1a0, CHAINS[0][0], False), swap(m1a1, CHAINS[1][0], False)]
    m1b0, own1, keep0, keep1, m1b1 = partials(
        ((1, 0, "q"), (1, 1, "f"), (0, 0, "f"), (0, 1, "f")), 1, tab, acts, og, rows, (m1b1,)
    )
    r1b = [swap(m1b0, CHAINS[0][0], False), swap(m1b1, CHAINS[1][0], False)]
    own, keep = [own0, own1], [keep0, keep1]

    msg8, msg4, msg2 = i16(8 * rows, half), i16(4 * rows, half), i16(2 * rows, half)
    four = (4, rows, half)
    kept4, r4 = [], []
    r2, r3 = [], []
    for c, (m1, m2) in enumerate(CHAINS):
        m2a, m2b = call(
            second_kernel,
            (own[c], r1a[c]),
            [whole((8, rows, half)), whole(msg8.shape)],
            [msg4, msg4],
            [pltpu.VMEM(four, F32)],
        )
        r2.append((swap(m2a, m2, False), swap(m2b, m2, False)))
    for c, (m1, m2) in enumerate(CHAINS):
        (m3,) = call(
            third_kernel,
            (keep[c], r1b[c], r2[c][0]),
            [whole(four), whole(msg4.shape), whole(msg4.shape)],
            [msg4],
            [pltpu.VMEM(four, F32)],
        )
        r3.append(swap(m3, m1, True))
    for c, (m1, m2) in enumerate(CHAINS):
        m4, k4 = call(
            fourth_kernel,
            (keep[c], r1b[c], r2[c][1], r3[c]),
            [whole(four, (1, 0, 0)), whole(msg8.shape), whole(msg4.shape), whole(msg4.shape)],
            [msg2, f32(2, rows, half)],
            [pltpu.VMEM((2, rows, half), F32)],
        )
        kept4.append(k4)
        r4.append(swap(m4, m2, True))
    m5, mine = call(
        fifth_kernel,
        (*kept4, *r4),
        [whole((2, rows, half))] * 2 + [whole(msg2.shape)] * 2,
        [i16(rows, width), f32(rows, width)],
    )
    r5 = lax.ppermute(m5, axes, far_pairs())
    groups = (rows // GROUP) * (width // GROUP)
    mom, kept = call(
        kept_kernel,
        (mine, r5, momentum, wa, wh, wl),
        [whole(a.shape) for a in (mine, r5, momentum, wa, wh, wl)],
        [f32(rows, width), f32(groups, n)],
    )
    total = kept
    for bit in (1, 2, 4):
        total = total + lax.ppermute(total, "rep", [(r, r ^ bit) for r in range(REPS)])
    (new_momentum,) = call(
        momentum_kernel,
        (mom, kept, wa, th, tl),
        [whole(a.shape) for a in (mom, kept, wa, th, tl)],
        [f32(rows, width)],
    )
    (update,) = call(
        update_kernel,
        (total, wa, th, tl),
        [whole(a.shape) for a in (total, wa, th, tl)],
        [f32(rows, width)],
    )
    return update, new_momentum[None]


def solution(mesh):
    return jax.shard_map(
        shards,
        mesh=mesh,
        in_specs=(P("rep", "fsdp", None), P("rep", "fsdp", None), P("rep", "fsdp", None), P()),
        out_specs=(P("fsdp", None), P("rep", "fsdp", None)),
        check_vma=False,
    )
```

```python
import functools

import jax
import jax.numpy as jnp
import numpy as np
from jax import lax
from jax.experimental import pallas as pl
from jax.experimental.pallas import tpu as pltpu
from jax.sharding import PartitionSpec as P

GROUP = 64
REPS = 8
DECAY = 0.999
HEAD = 16
STEPS = 256.0
TOP = 32766.0
LIMIT = 56 << 20
F32 = jnp.float32
I16 = jnp.int16
BF16 = jnp.bfloat16
CHAINS = ((1, 3), (3, 1))


def dct_table(order):
    n = np.arange(order)
    table = np.cos(np.pi * (2 * n[None, :] + 1) * n[:, None] / (2 * order)) * np.sqrt(2.0 / order)
    table[0] *= np.sqrt(0.5)
    return table.astype(np.float32)


def scale_code(biggest):
    top = jnp.max(biggest, axis=0, keepdims=True)
    return jnp.ceil(jnp.log2(jnp.maximum(top, 2.0**-110)) * STEPS)


def column_peak(x):
    return jnp.max(jnp.abs(x).reshape(x.shape[0] // 8, 8, x.shape[1]), axis=0)


def put_head(out, code):
    rows = jnp.broadcast_to(code, (HEAD, code.shape[1]))
    out[:HEAD, :] = rows.astype(jnp.int32).astype(I16)


def quantise(x, code):
    return jnp.round(x * (TOP * jnp.exp2(code * (-1.0 / STEPS)))).astype(jnp.int32).astype(I16)


def scale_of(msg):
    code = msg[:HEAD, :].astype(jnp.int32).astype(F32)[:1]
    return jnp.exp2(code * (1.0 / STEPS)) * (1.0 / TOP)


def dequantise(msg, block, rows, scale):
    return msg[HEAD + block * rows : HEAD + (block + 1) * rows, :].astype(jnp.int32).astype(F32) * scale


ORDERS = tuple((2, m1, m2, 0) for m1, m2 in CHAINS)


def pair_of(late, place, i):
    core, z, y, x = place // 32, (place // 16) % 2, (place // 4) % 4, place % 4
    first = core == 0
    u, v = jnp.where(first, x, y), jnp.where(first, y, x)
    zr, a, b = i // 4, (i // 2) % 2, i % 2
    far_half = (u // 2) ^ (1 - late)
    yd = jnp.where(first, 2 * a + b, 2 * far_half + a)
    xh = jnp.where(first, far_half, b)
    halves = []
    for s in range(2):
        xd = 2 * xh + s
        ud, vd = jnp.where(first, xd, yd), jnp.where(first, yd, xd)
        j = vd ^ v
        places = []
        for order in ORDERS:
            at = jnp.int32(0)
            for k, value in enumerate(order):
                at = jnp.where(j == value, k, at)
            places.append(at * 2 + zr)
        halves.append(((ud ^ u) % 2, places))
    return (z ^ zr) * 8 + yd * 2 + xh, halves


def partial_kernel(outs, late, passed, count, spot, acts, og, *rest):
    n = len(outs)
    here = spot[0]
    rest = rest[passed:]
    out_refs = rest[:n]
    pieces, acc, peak, ready, in_sems, out_sems = rest[n + passed :]
    rows, half = acc.shape[3:]

    def fetch(i):
        first = pl.multiple_of(pair_of(late, here, i)[0] * 2 * rows, 128)
        return pltpu.make_async_copy(acts.at[:, pl.ds(first, 2 * rows)], pieces.at[i], in_sems.at[i])

    for i in range(count):
        fetch(i).start()
    peak[...] = jnp.zeros_like(peak)

    @pl.loop(0, count)
    def _(i):
        fetch(i).wait()
        _, halves = pair_of(late, here, i)
        both = lax.dot_general(
            pieces[i], og[...], (((0,), (0,)), ((), ())), preferred_element_type=F32
        )
        for s in range(2):
            slot, places = halves[s]
            part = both[s * rows : (s + 1) * rows]
            peak[slot] = jnp.maximum(peak[slot], column_peak(part))
            for c in range(2):
                place = places[c]
                acc[c, slot, place] = part[:, c * half : (c + 1) * half]
                for k, (k_slot, k_c, kind) in enumerate(outs):
                    if kind == "f" and k_c == c:

                        @pl.when(slot == k_slot)
                        def _():
                            pltpu.make_async_copy(
                                acc.at[c, k_slot, place], out_refs[k].at[place], out_sems.at[k]
                            ).start()

    copies = []
    for k, (slot, c, kind) in enumerate(outs):
        if kind == "f":
            copies.append(pltpu.make_async_copy(acc.at[c, slot], out_refs[k], out_sems.at[k]))
    q = 0
    for k, (slot, c, kind) in enumerate(outs):
        if kind == "q":
            out = ready.at[q]
            code = scale_code(peak[slot][:, c * half : (c + 1) * half])
            put_head(out, code)
            for b in range(count):
                out[HEAD + b * rows : HEAD + (b + 1) * rows, :] = quantise(acc[c, slot, b], code)
            copies.append(pltpu.make_async_copy(out, out_refs[k], out_sems.at[k]))
            copies[-1].start()
            q += 1
    for copy in copies:
        copy.wait()


def partials(outs, late, spot, acts, og, rows, through=()):
    tokens, _ = acts.shape
    width = og.shape[1]
    half = width // 2
    count = acts.shape[1] // rows // 4
    shapes = [
        jax.ShapeDtypeStruct((HEAD + count * rows, half), I16) if kind == "q" else f32(count, rows, half)
        for _, _, kind in outs
    ]
    messages = sum(kind == "q" for _, _, kind in outs)
    anywhere = pl.BlockSpec(memory_space=pl.ANY)
    return pl.pallas_call(
        functools.partial(partial_kernel, outs, late, len(through), count),
        in_specs=[pl.BlockSpec(memory_space=pltpu.SMEM), anywhere, pl.BlockSpec(memory_space=pltpu.VMEM)]
        + [anywhere] * len(through),
        out_specs=[anywhere] * (len(outs) + len(through)),
        out_shape=shapes + [jax.ShapeDtypeStruct(t.shape, t.dtype) for t in through],
        input_output_aliases={3 + k: len(outs) + k for k in range(len(through))},
        scratch_shapes=[
            pltpu.VMEM((count, tokens, 2 * rows), BF16),
            pltpu.VMEM((2, 2, count, rows, half), F32),
            pltpu.VMEM((2, 8, width), F32),
            pltpu.VMEM((messages, HEAD + count * rows, half), I16),
            pltpu.SemaphoreType.DMA((count,)),
            pltpu.SemaphoreType.DMA((len(outs),)),
        ],
        compiler_params=pltpu.CompilerParams(vmem_limit_bytes=LIMIT),
        cost_estimate=pl.CostEstimate(
            flops=2 * tokens * count * 2 * rows * width, bytes_accessed=tokens * count * 2 * rows * 2, transcendentals=0
        ),
    )(spot, acts, og, *through)


def whole(shape, index=None):
    return pl.BlockSpec(shape, lambda i: index or (0,) * len(shape))


def call(kernel, ins, in_specs, outs, scratch=(), limit=16 << 20):
    total = sum(x.size * x.dtype.itemsize for x in ins) + sum(np.prod(o.shape) * o.dtype.itemsize for o in outs)
    return pl.pallas_call(
        kernel,
        grid=(1,),
        in_specs=in_specs,
        out_specs=[whole(o.shape) for o in outs],
        out_shape=outs,
        scratch_shapes=list(scratch),
        compiler_params=pltpu.CompilerParams(vmem_limit_bytes=limit),
        cost_estimate=pl.CostEstimate(flops=4 * int(total), bytes_accessed=int(total), transcendentals=0),
    )(*ins)


def i16(rows, width):
    return jax.ShapeDtypeStruct((HEAD + rows, width), I16)


def f32(*shape):
    return jax.ShapeDtypeStruct(shape, F32)


def second_kernel(start, own, first, *rest):
    out, held = rest[-2:]
    rows = own.shape[1]
    count = own.shape[0]
    scale = scale_of(first)
    peak = None
    for b in range(count):
        x = own[b] + dequantise(first, start + b, rows, scale)
        held[b] = x
        p = column_peak(x)
        peak = p if peak is None else jnp.maximum(peak, p)
    code = scale_code(peak)
    put_head(out, code)
    for b in range(count):
        out[HEAD + b * rows : HEAD + (b + 1) * rows, :] = quantise(held[b], code)


def third_kernel(own, near, far, out, held):
    rows = own.shape[1]
    n = own.shape[0]
    scale_n, scale_f = scale_of(near), scale_of(far)
    peak = None
    for b in range(n):
        x = own[b] + dequantise(near, b, rows, scale_n) + dequantise(far, b, rows, scale_f)
        held[b] = x
        p = column_peak(x)
        peak = p if peak is None else jnp.maximum(peak, p)
    code = scale_code(peak)
    put_head(out, code)
    for b in range(n):
        out[HEAD + b * rows : HEAD + (b + 1) * rows, :] = quantise(held[b], code)


def fourth_kernel(own, near, far, third, out, keep, held):
    rows = own.shape[1]
    n = own.shape[0]
    scale_n, scale_f, scale_t = scale_of(near), scale_of(far), scale_of(third)
    peak = None
    for b in range(n):
        x = own[b] + dequantise(near, n + b, rows, scale_n) + dequantise(far, b, rows, scale_f)
        x = x + dequantise(third, b, rows, scale_t)
        if b < n // 2:
            held[b] = x
            p = column_peak(x)
            peak = p if peak is None else jnp.maximum(peak, p)
        else:
            keep[b - n // 2] = x
    code = scale_code(peak)
    put_head(out, code)
    for b in range(n // 2):
        out[HEAD + b * rows : HEAD + (b + 1) * rows, :] = quantise(held[b], code)


def fifth_kernel(keep0, keep1, msg0, msg1, out, mine):
    rows = keep0.shape[1]
    half = keep0.shape[2]
    for c, (keep, msg) in enumerate(((keep0, msg0), (keep1, msg1))):
        cols = slice(c * half, (c + 1) * half)
        scale = scale_of(msg)
        mine[:, cols] = keep[0] + dequantise(msg, 0, rows, scale)
        x = keep[1] + dequantise(msg, 1, rows, scale)
        code = scale_code(column_peak(x))
        out[:HEAD, cols] = jnp.broadcast_to(code, (HEAD, half)).astype(jnp.int32).astype(I16)
        out[HEAD:, cols] = quantise(x, code)


def split(x):
    high = x.astype(BF16)
    return high, (x - high.astype(F32)).astype(BF16)


def mm(a, b):
    return jnp.dot(a, b, preferred_element_type=F32)


def waves_kernel(band, table, wa, wh, wl, th, tl):
    order = table.shape[0]
    n = band.shape[1]
    t = table[...]
    t0 = t.astype(BF16)
    r = t - t0.astype(F32)
    t1 = r.astype(BF16)
    t2 = (r - t1.astype(F32)).astype(BF16)
    ids = lax.broadcasted_iota(jnp.int32, (order, n), 0)
    pos = jnp.broadcast_to(band[...], (order, n))

    def pick(which):
        hot = jnp.where(ids == which, 1.0, 0.0).astype(BF16)
        return mm(t0, hot) + mm(t1, hot) + mm(t2, hot)

    left = pick(lax.shift_right_logical(pos, 6))
    right = pick(jnp.bitwise_and(pos, order - 1))
    for g in range(wa.shape[0] // order):
        wa[g * order : (g + 1) * order, :] = left
    high, low = split(right)
    for out, back, x in ((wh, th, high), (wl, tl, low)):
        x = x.astype(F32)
        zero = jnp.zeros_like(x)
        both = jnp.concatenate(
            [jnp.concatenate([x, zero], axis=1), jnp.concatenate([zero, x], axis=1)], axis=0
        )
        out[...] = both.astype(BF16)
        back[...] = both.T.astype(BF16)


def kept_kernel(mine, msg, momentum, wa, wh, wl, mom, kept):
    rows, width = mine.shape
    n = wa.shape[1]
    pairs = width // 128
    grad = mine[...] + msg[HEAD:, :].astype(jnp.int32).astype(F32) * scale_of(msg)
    now = DECAY * momentum[...] + grad
    mom[...] = now
    left = wa[...]
    for p in range(pairs):
        high, low = split(now[:, p * 128 : (p + 1) * 128])
        y = mm(high, wh[...]) + mm(low, wh[...]) + mm(high, wl[...])
        for h in range(2):
            z = left * y[:, h * n : (h + 1) * n]
            for g in range(rows // GROUP):
                row = g * 2 * pairs + 2 * p + h
                kept[row : row + 1, :] = jnp.sum(z[g * GROUP : (g + 1) * GROUP], axis=0, keepdims=True)


def back(values, wa, th, tl, store):
    n = wa.shape[1]
    groups = wa.shape[0] // GROUP
    pairs = values.shape[0] // groups // 2
    left = wa[:GROUP, :]
    for p in range(pairs):
        stacked = []
        for g in range(groups):
            row = g * 2 * pairs + 2 * p
            stacked.append(
                jnp.concatenate([left * values[row : row + 1], left * values[row + 1 : row + 2]], axis=1)
            )
        high, low = split(jnp.concatenate(stacked, axis=0))
        store(p, mm(high, th[...]) + mm(low, th[...]) + mm(high, tl[...]))


def momentum_kernel(mom, kept, wa, th, tl, out):
    def store(p, x):
        cols = slice(p * 128, (p + 1) * 128)
        out[:, cols] = mom[:, cols] - x

    back(kept[...], wa, th, tl, store)


def update_kernel(total, wa, th, tl, out):
    def store(p, x):
        out[:, p * 128 : (p + 1) * 128] = x

    back(total[...] * (1.0 / REPS), wa, th, tl, store)


def coords(f):
    return f // 16, (f // 4) % 4, f % 4


def partner_pairs(chain_step, late):
    pairs = []
    for rep in range(8):
        core = rep % 2
        for f in range(32):
            z, y, x = coords(f)
            if (core == 0) != late:
                x ^= chain_step
            else:
                y ^= chain_step
            pairs.append((rep * 32 + f, rep * 32 + z * 16 + y * 4 + x))
    return pairs


def far_pairs():
    return [(rep * 32 + f, rep * 32 + (f ^ 16)) for rep in range(8) for f in range(32)]


def shards(activations, out_grads, momentum, band):
    acts, og, momentum = activations[0], out_grads[0], momentum[0]
    rows, width = momentum.shape
    half = width // 2
    axes = ("rep", "fsdp")
    core = lax.axis_index("rep") % 2
    spot = (core * 32 + lax.axis_index("fsdp")).reshape(1)

    table = jnp.asarray(dct_table(GROUP).T)
    n = band.shape[0]
    wa, wh, wl, th, tl = call(
        waves_kernel,
        (band.reshape(1, n), table),
        [whole((1, n)), whole((GROUP, GROUP))],
        [f32(rows, n)]
        + [jax.ShapeDtypeStruct((128, 2 * n), BF16)] * 2
        + [jax.ShapeDtypeStruct((2 * n, 128), BF16)] * 2,
    )

    def swap(x, step, late):
        return lax.ppermute(x, axes, partner_pairs(step, late))

    m1a0, m1a1, m1b1, own0 = partials(((0, 0, "q"), (0, 1, "q"), (1, 1, "q"), (1, 0, "f")), 0, spot, acts, og, rows)
    r1a = [swap(m1a0, CHAINS[0][0], False), swap(m1a1, CHAINS[1][0], False)]
    m1b0, own1, keep0, keep1, m1b1 = partials(
        ((1, 0, "q"), (1, 1, "f"), (0, 0, "f"), (0, 1, "f")), 1, spot, acts, og, rows, (m1b1,)
    )
    r1b = [swap(m1b0, CHAINS[0][0], False), swap(m1b1, CHAINS[1][0], False)]
    own, keep = [own0, own1], [keep0, keep1]

    msg8, msg4, msg2 = i16(8 * rows, half), i16(4 * rows, half), i16(2 * rows, half)
    four = (4, rows, half)
    kept4, r4 = [], []
    r3 = []

    def second(c, part, after=()):
        (m,) = call(
            functools.partial(second_kernel, 4 * part),
            (own[c], r1a[c], *after),
            [whole(four, (part, 0, 0)), whole(msg8.shape)] + [pl.BlockSpec(memory_space=pl.ANY)] * len(after),
            [msg4],
            [pltpu.VMEM(four, F32)],
        )
        return swap(m, CHAINS[c][1], False)

    r2a = [second(c, 0) for c in range(2)]
    r2b = [second(c, 1, (r1b[1 - c],)) for c in range(2)]
    for c, (m1, m2) in enumerate(CHAINS):
        (m3,) = call(
            third_kernel,
            (keep[c], r1b[c], r2a[c]),
            [whole(four), whole(msg4.shape), whole(msg4.shape)],
            [msg4],
            [pltpu.VMEM(four, F32)],
        )
        r3.append(swap(m3, m1, True))
    for c, (m1, m2) in enumerate(CHAINS):
        m4, k4 = call(
            fourth_kernel,
            (keep[c], r1b[c], r2b[c], r3[c]),
            [whole(four, (1, 0, 0)), whole(msg8.shape), whole(msg4.shape), whole(msg4.shape)],
            [msg2, f32(2, rows, half)],
            [pltpu.VMEM((2, rows, half), F32)],
        )
        kept4.append(k4)
        r4.append(swap(m4, m2, True))
    m5, mine = call(
        fifth_kernel,
        (*kept4, *r4),
        [whole((2, rows, half))] * 2 + [whole(msg2.shape)] * 2,
        [i16(rows, width), f32(rows, width)],
    )
    r5 = lax.ppermute(m5, axes, far_pairs())
    groups = (rows // GROUP) * (width // GROUP)
    mom, kept = call(
        kept_kernel,
        (mine, r5, momentum, wa, wh, wl),
        [whole(a.shape) for a in (mine, r5, momentum, wa, wh, wl)],
        [f32(rows, width), f32(groups, n)],
    )
    total = kept
    for bit in (1, 2, 4):
        total = total + lax.ppermute(total, "rep", [(r, r ^ bit) for r in range(REPS)])
    (new_momentum,) = call(
        momentum_kernel,
        (mom, kept, wa, th, tl),
        [whole(a.shape) for a in (mom, kept, wa, th, tl)],
        [f32(rows, width)],
    )
    (update,) = call(
        update_kernel,
        (total, wa, th, tl),
        [whole(a.shape) for a in (total, wa, th, tl)],
        [f32(rows, width)],
    )
    return update, new_momentum[None]


def solution(mesh):
    return jax.shard_map(
        shards,
        mesh=mesh,
        in_specs=(P("rep", "fsdp", None), P("rep", "fsdp", None), P("rep", "fsdp", None), P()),
        out_specs=(P("fsdp", None), P("rep", "fsdp", None)),
        check_vma=False,
    )
```
